32 devices in a mesh: groups: 2 (over x), row: 8 (over z, y), col: 2 (over core).
Axes of the slice: x: 2, y: 2, z: 4, core: 2. Of those that a mesh axis runs over, the one named last changes fastest.
Arguments:
- pair: bfloat16 [384, 192, 128], P(('groups', 'row'), 'col'), parts along dimension 0, may hold values from -6 to 6
- mask: int32 [384, 192], P(('groups', 'row'), 'col'), parts along dimension 0, may hold values from 0 to 1, as said below
- w_in: bfloat16 [2, 128, 512], replicated, may hold values from -0.5 to 0.5
- w_gate: bfloat16 [2, 128, 128], replicated, may hold values from -0.5 to 0.5
- w_out: bfloat16 [2, 128, 128], replicated, may hold values from -0.5 to 0.5
Outputs:
- pair_out: bfloat16 [384, 192, 128], P(('groups', 'row'), 'col'), parts along dimension 0
The draws below stay inside these ranges and needn't reach their ends.
There are 2 independent parts, one for each index of `groups`. The reference program is written for one: setup_inputs(seed, part) draws one part's arguments, and reference() takes and returns one part's arrays. A program takes and returns all parts, laid end to end along the dimension named above; an argument that names none is the same for every part. Nothing has to cross between parts.
Inputs may be any that keep to these rules, and one draw needn't show every extreme that they name: mask[i][j] is 1 exactly when residues i and j are both real. The residues fall into four chain slots of 48 in order; in each slot the real residues run from the slot's start for the chain's length, at least 24, and the rest are padding.
All inputs are finite; a program needn't handle non-finite values.
Results may differ from the reference program's by a relative error of at most 0.012.
Values may be sent and summed in bfloat16 or wider, within the bound.
A program may use at most 128 MiB of HBM per device.

```python
import jax
import jax.numpy as jnp
from jax import lax

C = 128
H = 128
RESIDUES = 192


def draw_mask(key, part):
    key = jax.random.fold_in(key, 11)
    slot_size = RESIDUES // 4
    lengths = jax.random.randint(key, (4,), slot_size // 2, slot_size + 1)
    position = jnp.arange(RESIDUES, dtype=jnp.int32)
    is_real = position % slot_size < lengths[position // slot_size]
    return (is_real[:, None] & is_real[None, :]).astype(jnp.int32)


def steps_of(own_key, dims, shards, smallest, top_value):
    def one(axis_at, blocks):
        heights = jax.random.uniform(jax.random.fold_in(jax.random.fold_in(own_key, 6), axis_at), (blocks,), jnp.float32, smallest / len(shards), top_value / len(shards))
        return jnp.repeat(jnp.exp(heights), dims[axis_at] // blocks).reshape((-1,) + (1,) * (len(dims) - axis_at - 1))

    gain = one(*shards[0])
    for cut in shards[1:]:
        gain = gain * one(*cut)
    return gain


def bell_draw(own_key, extent, spread, most, pieces=(), kind=jnp.bfloat16):
    array = spread * jax.random.normal(own_key, extent, jnp.float32)
    if pieces:
        array = array * steps_of(own_key, extent, pieces, -0.22, 0.18)
    return jnp.clip(array, -most, most).astype(kind)


def setup_inputs(seed: int = 0, part: int = 0) -> dict:
    arg_keys = jax.random.split(jax.random.key(seed), 6)
    part_keys = jax.random.split(jax.random.fold_in(arg_keys[5], part), 6)
    return {
        "pair": bell_draw(part_keys[0], (RESIDUES, RESIDUES, C), 1.0, 6.0, ((0, 8), (1, 2))),
        "mask": draw_mask(jax.random.fold_in(jax.random.fold_in(arg_keys[5], part), 71), part),
        "w_in": bell_draw(arg_keys[2], (2, C, 4 * H), C ** -0.5, 0.5),
        "w_gate": bell_draw(arg_keys[3], (2, C, C), C ** -0.5, 0.5),
        "w_out": bell_draw(arg_keys[4], (2, H, C), H ** -0.5, 0.5),
    }


def layer_norm(values, dimension):
    average = lax.optimization_barrier(jnp.mean(values, axis=dimension, keepdims=True))
    centered = values - average
    variance = lax.optimization_barrier(jnp.mean(centered * centered, axis=dimension, keepdims=True))
    return centered * lax.rsqrt(variance + 1e-05)

def triangle(pair_in, mask_flat, weight_in, weight_gate, weight_out, outgoing):
    flat_pair = pair_in.reshape(RESIDUES * RESIDUES, C).astype(jnp.float32)
    normed = layer_norm(flat_pair, 1).astype(jnp.bfloat16)
    gate_logits = jnp.dot(normed, weight_in[:, :2 * H], preferred_element_type=jnp.float32)
    values = jnp.dot(normed, weight_in[:, 2 * H:], preferred_element_type=jnp.float32)
    stacked = (mask_flat[:, None] * jax.nn.sigmoid(gate_logits) * values).astype(jnp.bfloat16)
    stacked = stacked.reshape(RESIDUES, RESIDUES, 2, H // 8, 8)
    stacked = jnp.transpose(stacked, (3, 2, 4, 0, 1))
    equation = 'mik,mjk->mij' if outgoing else 'mki,mkj->mij'

    def contract_block(block_pair):
        left_part = block_pair[0].astype(jnp.float32)
        right_part = block_pair[1].astype(jnp.float32)
        return jnp.einsum(equation, left_part, right_part).astype(jnp.bfloat16)
    mixed = lax.map(contract_block, stacked).reshape(H, RESIDUES, RESIDUES)
    mixed = jnp.transpose(mixed, (1, 2, 0)).reshape(RESIDUES * RESIDUES, H)
    mixed_norm = layer_norm(mixed.astype(jnp.float32), 1).astype(jnp.bfloat16)
    update = jnp.dot(mixed_norm, weight_out, preferred_element_type=jnp.float32)
    gate_value = jax.nn.sigmoid(jnp.dot(normed, weight_gate, preferred_element_type=jnp.float32))
    result = (flat_pair + gate_value * update).astype(jnp.bfloat16)
    return result.reshape(RESIDUES, RESIDUES, C)

def reference(pair, mask, w_in, w_gate, w_out):
    mask_flat = mask.reshape(RESIDUES * RESIDUES).astype(jnp.float32)
    first = triangle(pair, mask_flat, w_in[0], w_gate[0], w_out[0], True)
    return triangle(first, mask_flat, w_in[1], w_gate[1], w_out[1], False)
```

```python
import functools

import jax
import jax.numpy as jnp
from jax import lax
from jax.experimental import pallas as pl
from jax.experimental.pallas import tpu as pltpu
from jax.sharding import PartitionSpec as P

LANES = 128


def layer_norm(values, dimension):
    average = jnp.mean(values, axis=dimension, keepdims=True)
    centered = values - average
    variance = jnp.mean(centered * centered, axis=dimension, keepdims=True)
    return centered * lax.rsqrt(variance + 1e-05)


def triangle(pair_in, mask_flat, weight_in, weight_gate, weight_out, outgoing):
    tile_rows, tile_cols, channels = pair_in.shape
    pair_count = tile_rows * tile_cols
    hidden = weight_in.shape[1] // 4
    row_count = lax.axis_size("row")
    col_count = lax.axis_size("col")
    groups = row_count * col_count
    per_group = hidden // groups
    flat_pair = pair_in.reshape(pair_count, channels).astype(jnp.float32)
    normed = layer_norm(flat_pair, 1).astype(jnp.bfloat16)
    projected = jnp.einsum("pc,ch->hp", normed, weight_in, preferred_element_type=jnp.float32)
    stacked = (
        mask_flat[None, :] * jax.nn.sigmoid(projected[: 2 * hidden]) * projected[2 * hidden :]
    ).astype(jnp.bfloat16)
    stacked = stacked.reshape(2, groups, per_group, pair_count)
    equation = "mik,mjk->mij" if outgoing else "mki,mkj->mij"
    pieces = lax.all_to_all(stacked, ("row", "col"), split_axis=1, concat_axis=1, tiled=True)
    item_count = pieces.shape[2]
    gathered = pieces.reshape(2, row_count, col_count, item_count, tile_rows, tile_cols)
    gathered = jnp.transpose(gathered, (0, 3, 1, 4, 2, 5))
    gathered = gathered.reshape(2, item_count, row_count * tile_rows, col_count * tile_cols)
    product = jnp.einsum(
        equation, gathered[0], gathered[1], preferred_element_type=jnp.float32
    ).astype(jnp.bfloat16)
    product = product.reshape(item_count, row_count, tile_rows, col_count, tile_cols)
    product = jnp.transpose(product, (1, 3, 0, 2, 4))
    result = lax.all_to_all(
        product.reshape(groups, item_count, pair_count),
        ("row", "col"),
        split_axis=0,
        concat_axis=0,
        tiled=True,
    )
    result = result.reshape(hidden, pair_count)
    mixed_norm = layer_norm(result.astype(jnp.float32), 0).astype(jnp.bfloat16)
    update = jnp.einsum("hp,hc->pc", mixed_norm, weight_out, preferred_element_type=jnp.float32)
    gate_value = jax.nn.sigmoid(jnp.dot(normed, weight_gate, preferred_element_type=jnp.float32))
    output = (flat_pair + gate_value * update).astype(jnp.bfloat16)
    return output.reshape(tile_rows, tile_cols, channels)


def flip(index, step, count):
    total, bit = 0, 1
    while bit < count:
        total = total + ((index // bit + step // bit) % 2) * bit
        bit *= 2
    return total


def step_order(count):
    half = count // 2
    return [half + k // 2 if k % 2 == 0 else (k // 2 + 1) % half for k in range(count)]


def fused_kernel(
    outgoing, rows, cols, T, W,
    z_ref, mask_ref, win_ref, wgate_ref, wout_ref, out_ref,
    normed, normed_t, gate, send1, recv1, pairs, mix, send2, recv2, mixed_t,
    send_sem1, recv_sem1, send_sem2, recv_sem2,
):
    D = rows * cols
    count = T * W
    C = z_ref.shape[1]
    owned = recv1.shape[1] // 2
    N = rows * T
    per_col = N // cols
    me = lax.axis_index("row") * cols + lax.axis_index("col")
    order = step_order(D)
    lane = lax.broadcasted_iota(jnp.int32, (1, LANES), 1)

    def device(step):
        other = flip(me, step, D)
        return {"row": other // cols, "col": other % cols}

    barrier = pltpu.get_barrier_semaphore()
    for step in range(1, D):
        pl.semaphore_signal(
            barrier, inc=1, device_id=device(step), device_id_type=pl.DeviceIdType.MESH
        )

    chunk = 384
    chunks = count // chunk

    def normalize(part, carry):
        at = pl.ds(pl.multiple_of(part * chunk, chunk), chunk)
        values = z_ref[at, :].astype(jnp.float32)
        centered = values - jnp.mean(values, axis=1, keepdims=True)
        variance = jnp.mean(centered * centered, axis=1, keepdims=True)
        result = centered * lax.rsqrt(variance + 1e-05)
        normed[at, :] = result.astype(jnp.bfloat16)
        normed_t[:, at] = result.T.astype(jnp.bfloat16)
        return carry

    lax.fori_loop(0, chunks, normalize, 0)
    pl.semaphore_wait(barrier, D - 1)

    def copy1(step):
        return pltpu.make_async_remote_copy(
            src_ref=send1.at[step],
            dst_ref=recv1.at[step],
            send_sem=send_sem1.at[step],
            recv_sem=recv_sem1.at[step],
            device_id=device(step),
            device_id_type=pl.DeviceIdType.MESH,
        )

    def copy2(step):
        return pltpu.make_async_remote_copy(
            src_ref=send2.at[step],
            dst_ref=recv2.at[step],
            send_sem=send_sem2.at[step],
            recv_sem=recv_sem2.at[step],
            device_id=device(step),
            device_id_type=pl.DeviceIdType.MESH,
        )

    bundle = 4
    wide = 768
    for first in range(0, D, bundle):
        steps = order[first : first + bundle]
        weights = jnp.concatenate([win_ref[flip(me, step, D)] for step in steps], axis=0)
        for start in range(0, count, wide):
            here = pl.ds(start, wide)
            projected = jnp.dot(weights, normed_t[:, here], preferred_element_type=jnp.float32)
            for place, step in enumerate(steps):
                base = place * 4 * owned
                gates = projected[base : base + 2 * owned]
                values = projected[base + 2 * owned : base + 4 * owned]
                opened = 0.5 + 0.5 * jnp.tanh(0.5 * gates)
                target = recv1 if step == 0 else send1
                target[step, :, here] = (mask_ref[:, here] * opened * values).astype(jnp.bfloat16)
        for step in steps:
            if step:
                copy1(step).start()

    def open_gate(part, carry):
        at = pl.ds(pl.multiple_of(part * chunk, chunk), chunk)
        logits = jnp.dot(normed[at, :], wgate_ref[...], preferred_element_type=jnp.float32)
        gate[at, :] = 0.5 + 0.5 * jnp.tanh(0.5 * logits)
        return carry

    lax.fori_loop(0, chunks, open_gate, 0)

    def spread(step):
        source = flip(me, step, D)
        block, half = source // cols, source % cols
        for four in range(T // 4):
            v = [
                recv1[step, :, pl.ds((3 * four + i) * LANES, LANES)].astype(jnp.float32)
                for i in range(3)
            ]
            pieces = [
                v[0],
                jnp.where(lane < 32, pltpu.roll(v[0], 32, 1), pltpu.roll(v[1], 32, 1)),
                jnp.where(lane < 64, pltpu.roll(v[1], 64, 1), pltpu.roll(v[2], 64, 1)),
                pltpu.roll(v[2], 96, 1),
            ]
            for i, piece in enumerate(pieces):
                pairs[half, block, pl.ds(4 * four + i, 2 * owned, stride=T), :] = jnp.where(
                    lane < W, piece, 0.0
                )

    spread(0)

    def receive(k, carry):
        step = jnp.where(k % 2 == 0, D // 2 + k // 2, (k // 2 + 1) % (D // 2))
        copy1(step).wait_recv()
        spread(step)
        return carry

    lax.fori_loop(0, D - 1, receive, 0)

    def channel(which, half):
        block = pairs[half, :, pl.ds(which * T, T), :]
        return block.reshape(N, LANES).astype(jnp.bfloat16)

    for h in range(owned):
        left = jnp.concatenate([channel(h, half) for half in range(cols)], axis=1)
        right = jnp.concatenate([channel(owned + h, half) for half in range(cols)], axis=1)
        if outgoing:
            blank = jnp.zeros((LANES - per_col, cols * LANES), jnp.bfloat16)
            parts = []
            for half in range(cols):
                parts += [right[half * per_col : (half + 1) * per_col], blank]
            right = jnp.concatenate(parts, axis=0)
            product = lax.dot_general(
                left, right, (((1,), (1,)), ((), ())), preferred_element_type=jnp.float32
            )
        else:
            product = lax.dot_general(
                left, right, (((0,), (0,)), ((), ())), preferred_element_type=jnp.float32
            )
        for block in range(rows):
            at = block * T
            if not outgoing:
                at = at // per_col * LANES + at % per_col
            for half in range(cols):
                mix[block, half, pl.ds(h * T, T), :] = product[
                    at : at + T, half * LANES : (half + 1) * LANES
                ]

    def pack(step, target):
        other = flip(me, step, D)
        block, half = other // cols, other % cols
        for four in range(T // 8):
            both = []
            for upper in range(2):
                row = upper * (T // 2) + 4 * four
                p = [
                    mix[block, half, pl.ds(row + i, owned, stride=T), :] for i in range(4)
                ]
                one, two, three = pltpu.roll(p[1], 96, 1), pltpu.roll(p[2], 64, 1), pltpu.roll(p[3], 32, 1)
                both.append([
                    jnp.where(lane < 96, p[0], one),
                    jnp.where(lane < 64, one, two),
                    jnp.where(lane < 32, two, three),
                ])
            for i in range(3):
                target[step, :, pl.ds((3 * four + i) * LANES, LANES)] = jnp.concatenate(
                    [both[0][i], both[1][i]], axis=0
                ).astype(jnp.bfloat16)

    def give(k, carry):
        step = jnp.where(k % 2 == 0, D // 2 + k // 2, (k // 2 + 1) % (D // 2))
        pack(step, send2)
        copy2(step).start()
        return carry

    lax.fori_loop(0, D - 1, give, 0)
    pack(0, recv2)

    def collect(step):
        owner = flip(me, step, D)
        values = recv2[step].astype(jnp.float32)
        mixed_t[owner, :, : count // 2] = values[:owned]
        mixed_t[owner, :, count // 2 :] = values[owned:]

    collect(0)

    def take(k, carry):
        step = jnp.where(k % 2 == 0, D // 2 + k // 2, (k // 2 + 1) % (D // 2))
        copy2(step).wait_recv()
        collect(step)
        return carry

    lax.fori_loop(0, D - 1, take, 0)

    def finish(part, carry):
        at = pl.ds(pl.multiple_of(part * chunk, chunk), chunk)
        values = mixed_t[:, :, at].reshape(D * owned, chunk)
        centered = values - jnp.mean(values, axis=0, keepdims=True)
        variance = jnp.mean(centered * centered, axis=0, keepdims=True)
        mixed_norm = (centered * lax.rsqrt(variance + 1e-05)).T.astype(jnp.bfloat16)
        update = jnp.dot(mixed_norm, wout_ref[...], preferred_element_type=jnp.float32)
        out_ref[at, :] = (z_ref[at, :].astype(jnp.float32) + gate[at, :] * update).astype(jnp.bfloat16)
        return carry

    lax.fori_loop(0, chunks, finish, 0)

    def settle(step, carry):
        copy1(step).wait_send()
        copy2(step).wait_send()
        return carry

    lax.fori_loop(1, D, settle, 0)


def fused_triangle(flat, mask_flat, weight_in, weight_gate, weight_out, outgoing, T, W):
    rows, cols = lax.axis_size("row"), lax.axis_size("col")
    D = rows * cols
    count, C = flat.shape
    owned = weight_in.shape[1] // 4
    vmem = pltpu.VMEM
    return pl.pallas_call(
        functools.partial(fused_kernel, outgoing, rows, cols, T, W),
        out_shape=jax.ShapeDtypeStruct((count, C), jnp.bfloat16),
        in_specs=[pl.BlockSpec(memory_space=vmem)] * 5,
        out_specs=pl.BlockSpec(memory_space=vmem),
        scratch_shapes=[
            vmem((count, C), jnp.bfloat16),
            vmem((C, count), jnp.bfloat16),
            vmem((count, C), jnp.float32),
            vmem((D, 2 * owned, count), jnp.bfloat16),
            vmem((D, 2 * owned, count), jnp.bfloat16),
            vmem((cols, rows, 2 * owned * T, LANES), jnp.float32),
            vmem((rows, cols, owned * T, LANES), jnp.float32),
            vmem((D, 2 * owned, count // 2), jnp.bfloat16),
            vmem((D, 2 * owned, count // 2), jnp.bfloat16),
            vmem((D, owned, count), jnp.float32),
            pltpu.SemaphoreType.DMA((D,)),
            pltpu.SemaphoreType.DMA((D,)),
            pltpu.SemaphoreType.DMA((D,)),
            pltpu.SemaphoreType.DMA((D,)),
        ],
        compiler_params=pltpu.CompilerParams(
            collective_id=0 if outgoing else 1,
            has_side_effects=True,
            vmem_limit_bytes=48 * 1024 * 1024,
        ),
    )(flat, mask_flat, weight_in, weight_gate, weight_out)


def fits_fused(pair, w_in):
    rows, cols = lax.axis_size("row"), lax.axis_size("col")
    D = rows * cols
    T, W, C = pair.shape
    H = w_in.shape[2] // 4
    return (
        W == 96 and T % 8 == 0 and cols == 2 and D & (D - 1) == 0
        and C == LANES and H == LANES and H == 8 * D and rows * T == cols * W
    )


def per_device(pair, mask, w_in, w_gate, w_out):
    mask_flat = mask.reshape(-1).astype(jnp.float32)
    if fits_fused(pair, w_in):
        T, W, C = pair.shape
        D = lax.axis_size("row") * lax.axis_size("col")
        H = w_in.shape[2] // 4
        by_owner = w_in.reshape(2, C, 4, D, H // D)
        by_owner = jnp.transpose(by_owner, (0, 3, 2, 4, 1)).reshape(2, D, 4 * H // D, C)
        values = pair.reshape(T * W, C)
        for update in range(2):
            values = fused_triangle(
                values, mask_flat[None, :], by_owner[update], w_gate[update], w_out[update],
                update == 0, T, W,
            )
        return values.reshape(T, W, C)
    first = triangle(pair, mask_flat, w_in[0], w_gate[0], w_out[0], True)
    return triangle(first, mask_flat, w_in[1], w_gate[1], w_out[1], False)


def solution(mesh):
    placed = (P(("groups", "row"), "col", None), P(("groups", "row"), "col"), P(), P(), P())
    return jax.shard_map(
        per_device,
        mesh=mesh,
        in_specs=placed,
        out_specs=P(("groups", "row"), "col", None),
        check_vma=False,
    )
```

```python
import functools

import jax
import jax.numpy as jnp
from jax import lax
from jax.experimental import pallas as pl
from jax.experimental.pallas import tpu as pltpu
from jax.sharding import PartitionSpec as P

LANES = 128


def layer_norm(values, dimension):
    average = jnp.mean(values, axis=dimension, keepdims=True)
    centered = values - average
    variance = jnp.mean(centered * centered, axis=dimension, keepdims=True)
    return centered * lax.rsqrt(variance + 1e-05)


def triangle(pair_in, mask_flat, weight_in, weight_gate, weight_out, outgoing):
    tile_rows, tile_cols, channels = pair_in.shape
    pair_count = tile_rows * tile_cols
    hidden = weight_in.shape[1] // 4
    row_count = lax.axis_size("row")
    col_count = lax.axis_size("col")
    groups = row_count * col_count
    per_group = hidden // groups
    flat_pair = pair_in.reshape(pair_count, channels).astype(jnp.float32)
    normed = layer_norm(flat_pair, 1).astype(jnp.bfloat16)
    projected = jnp.einsum("pc,ch->hp", normed, weight_in, preferred_element_type=jnp.float32)
    stacked = (
        mask_flat[None, :] * jax.nn.sigmoid(projected[: 2 * hidden]) * projected[2 * hidden :]
    ).astype(jnp.bfloat16)
    stacked = stacked.reshape(2, groups, per_group, pair_count)
    equation = "mik,mjk->mij" if outgoing else "mki,mkj->mij"
    pieces = lax.all_to_all(stacked, ("row", "col"), split_axis=1, concat_axis=1, tiled=True)
    item_count = pieces.shape[2]
    gathered = pieces.reshape(2, row_count, col_count, item_count, tile_rows, tile_cols)
    gathered = jnp.transpose(gathered, (0, 3, 1, 4, 2, 5))
    gathered = gathered.reshape(2, item_count, row_count * tile_rows, col_count * tile_cols)
    product = jnp.einsum(
        equation, gathered[0], gathered[1], preferred_element_type=jnp.float32
    ).astype(jnp.bfloat16)
    product = product.reshape(item_count, row_count, tile_rows, col_count, tile_cols)
    product = jnp.transpose(product, (1, 3, 0, 2, 4))
    result = lax.all_to_all(
        product.reshape(groups, item_count, pair_count),
        ("row", "col"),
        split_axis=0,
        concat_axis=0,
        tiled=True,
    )
    result = result.reshape(hidden, pair_count)
    mixed_norm = layer_norm(result.astype(jnp.float32), 0).astype(jnp.bfloat16)
    update = jnp.einsum("hp,hc->pc", mixed_norm, weight_out, preferred_element_type=jnp.float32)
    gate_value = jax.nn.sigmoid(jnp.dot(normed, weight_gate, preferred_element_type=jnp.float32))
    output = (flat_pair + gate_value * update).astype(jnp.bfloat16)
    return output.reshape(tile_rows, tile_cols, channels)


def flip(index, step, count):
    total, bit = 0, 1
    while bit < count:
        total = total + ((index // bit + step // bit) % 2) * bit
        bit *= 2
    return total


def step_order(count):
    half = count // 2
    return [half + k // 2 if k % 2 == 0 else (k // 2 + 1) % half for k in range(count)]


def fused_kernel(
    rows, cols, T, W,
    z_ref, mask_ref, win_ref, wgate_ref, wout_ref, out_ref,
    mask_rows, mask_flat, weights0, weights1, between, normed_t, gate, mixed_t, pairs,
    send0, near0, far0, mix0, send0m, recv0m,
    send1, recv1, mix1, send1m, recv1m,
    near_send, near_recv, far_send, far_recv, back0_send, back0_recv,
    out1_send, out1_recv, back1_send, back1_recv,
):
    D = rows * cols
    local = D // 2
    count = T * W
    part = count // 2
    owned = recv1.shape[2] // 2
    N = rows * T
    per_col = N // cols
    fours = T // 4
    me = lax.axis_index("row") * cols + lax.axis_index("col")
    order = step_order(D)
    lane = lax.broadcasted_iota(jnp.int32, (1, LANES), 1)
    chunk = 384

    def device(step):
        other = flip(me, step, D)
        return {"row": other // cols, "col": other % cols}

    def remote(source, target, sent, received, step):
        return pltpu.make_async_remote_copy(
            src_ref=source, dst_ref=target, send_sem=sent, recv_sem=received,
            device_id=device(step), device_id_type=pl.DeviceIdType.MESH,
        )

    def near(t):
        return remote(send0.at[t], near0.at[t], near_send.at[t], near_recv.at[t], t)

    def far(t):
        return remote(
            send0.at[t, pl.ds(0, 2 * owned)], far0.at[t], far_send.at[t], far_recv.at[t], local + t
        )

    def back0(ph, t):
        return remote(
            send0m.at[ph, t], recv0m.at[ph, t], back0_send.at[ph, t], back0_recv.at[ph, t], t
        )

    def out1(ph, step):
        return remote(
            send1.at[ph, step], recv1.at[ph, step], out1_send.at[ph, step], out1_recv.at[ph, step], step
        )

    def back1(step):
        return remote(send1m.at[step], recv1m.at[step], back1_send.at[step], back1_recv.at[step], step)

    barrier = pltpu.get_barrier_semaphore()
    for step in range(1, D):
        pl.semaphore_signal(
            barrier, inc=1, device_id=device(step), device_id_type=pl.DeviceIdType.MESH
        )

    def split_rows(v):
        one = jnp.where(lane < 32, pltpu.roll(v[0], 32, 1), pltpu.roll(v[1], 32, 1))
        two = jnp.where(lane < 64, pltpu.roll(v[1], 64, 1), pltpu.roll(v[2], 64, 1))
        return [jnp.where(lane < W, x, 0.0) for x in (v[0], one, two, pltpu.roll(v[2], 96, 1))]

    def join_rows(p):
        one, two, three = pltpu.roll(p[1], 96, 1), pltpu.roll(p[2], 64, 1), pltpu.roll(p[3], 32, 1)
        return [
            jnp.where(lane < 96, p[0], one),
            jnp.where(lane < 64, one, two),
            jnp.where(lane < 32, two, three),
        ]

    def spread(load, half, block, begin, end):
        for four in range(begin, end):
            v = [load((3 * (four - begin) + i) * LANES).astype(jnp.float32) for i in range(3)]
            for i, piece in enumerate(split_rows(v)):
                pairs[half, block, pl.ds(4 * four + i, 2 * owned, stride=T), :] = piece

    def opened(logits):
        return 0.5 + 0.5 * jnp.tanh(0.5 * logits)

    def arrange(update, target, size):
        turned = win_ref[update].astype(jnp.float32).T
        H = turned.shape[0] // 4
        for owner in range(H // size):
            target[owner] = jnp.concatenate(
                [turned[q * H + owner * size : q * H + (owner + 1) * size] for q in range(4)], axis=0
            ).astype(jnp.bfloat16)

    def normalize(update, at, values):
        centered = values - jnp.mean(values, axis=1, keepdims=True)
        variance = jnp.mean(centered * centered, axis=1, keepdims=True)
        result = centered * lax.rsqrt(variance + 1e-05)
        normed_t[:, at] = result.T.astype(jnp.bfloat16)
        gate[at, :] = opened(
            jnp.dot(result.astype(jnp.bfloat16), wgate_ref[update], preferred_element_type=jnp.float32)
        )

    def normalize_input(index, carry):
        at = pl.ds(pl.multiple_of(index * chunk, chunk), chunk)
        normalize(0, at, z_ref[at, :].astype(jnp.float32))
        return carry

    arrange(0, weights0, 2 * owned)
    mask_rows[...] = jnp.zeros_like(mask_rows)
    mask_rows[:, :W] = mask_ref[...].astype(jnp.float32)
    for four in range(fours):
        p = [mask_rows[pl.ds(4 * four + i, 1), :] for i in range(4)]
        for i, piece in enumerate(join_rows(p)):
            mask_flat[:, pl.ds((3 * four + i) * LANES, LANES)] = piece
    lax.fori_loop(0, count // chunk, normalize_input, 0)
    pl.semaphore_wait(barrier, D - 1)

    wide = 768
    for first in range(0, local, 2):
        steps = (first, first + 1)
        weights = jnp.concatenate([weights0[flip(me, t, D) % local] for t in steps], axis=0)
        for start in range(0, count, wide):
            here = pl.ds(start, wide)
            projected = jnp.dot(weights, normed_t[:, here], preferred_element_type=jnp.float32)
            for place, t in enumerate(steps):
                base = place * 8 * owned
                gates = projected[base : base + 4 * owned]
                values = projected[base + 4 * owned : base + 8 * owned]
                both = (mask_flat[:, here] * opened(gates) * values).astype(jnp.bfloat16)
                send0[t, : 2 * owned, here] = both[2 * owned :]
                send0[t, 2 * owned :, here] = both[: 2 * owned]
        for t in steps:
            far(t).start()
        for t in steps:
            if t:
                near(t).start()

    def spread_near(ref, t):
        source = flip(me, t, D)
        block, half = source // cols, source % cols
        spread(lambda at: ref[t, : 2 * owned, pl.ds(at, LANES)], half, block, 0, fours)
        spread(
            lambda at: ref[t, 2 * owned :, pl.ds(at, LANES)],
            half, rows + block % (rows // 2), 0, fours,
        )

    def spread_far(t):
        far(t).wait_recv()
        source = flip(me, local + t, D)
        spread(
            lambda at: far0[t, :, pl.ds(at, LANES)], source % cols, source // cols, 0, fours
        )

    spread_near(send0, 0)
    arrange(1, weights1, owned)
    spread_far(0)

    def receive0(t, carry):
        near(t).wait_recv()
        spread_near(near0, t)
        spread_far(t)
        return carry

    lax.fori_loop(1, local, receive0, 0)

    def channel(which, half, begin, blocks):
        block = pairs[half, pl.ds(begin, blocks), pl.ds(which * T, T), :]
        return block.reshape(blocks * T, LANES).astype(jnp.bfloat16)

    for h in range(2 * owned):
        left = jnp.concatenate(
            [channel(h, half, rows, rows // 2) for half in range(cols)], axis=1
        )
        right = jnp.concatenate([channel(h, half, 0, rows) for half in range(cols)], axis=1)
        blank = jnp.zeros((LANES - per_col, cols * LANES), jnp.bfloat16)
        padded = []
        for half in range(cols):
            padded += [right[half * per_col : (half + 1) * per_col], blank]
        product = lax.dot_general(
            left, jnp.concatenate(padded, axis=0), (((1,), (1,)), ((), ())),
            preferred_element_type=jnp.float32,
        )
        for block in range(rows // 2):
            for half in range(cols):
                mix0[block, half, pl.ds(h * T, T), :] = product[
                    block * T : (block + 1) * T, half * LANES : (half + 1) * LANES
                ]

    def pack0(ph, t, target):
        other = flip(me, t, D)
        block, half = other // cols % (rows // 2), other % cols
        for four in range(fours // 2):
            row = ph * (T // 2) + 4 * four
            p = [mix0[block, half, pl.ds(row + i, 2 * owned, stride=T), :] for i in range(4)]
            for i, piece in enumerate(join_rows(p)):
                target[ph, t, :, pl.ds((3 * four + i) * LANES, LANES)] = piece.astype(jnp.bfloat16)

    for ph in range(2):
        def give0(t, carry):
            pack0(ph, t, send0m)
            back0(ph, t).start()
            return carry

        lax.fori_loop(1, local, give0, 0)
        pack0(ph, 0, recv0m)

    def mixed_update(update, at):
        values = mixed_t[:, at]
        centered = values - jnp.mean(values, axis=0, keepdims=True)
        variance = jnp.mean(centered * centered, axis=0, keepdims=True)
        mixed_norm = (centered * lax.rsqrt(variance + 1e-05)).T.astype(jnp.bfloat16)
        return gate[at, :] * jnp.dot(
            mixed_norm, wout_ref[update], preferred_element_type=jnp.float32
        )

    bundle = 4
    for ph in range(2):
        span = pl.ds(ph * part, part)

        def collect0(t):
            owner = flip(me, t, D) % local
            at = pl.ds(pl.multiple_of(owner * 2 * owned, 2 * owned), 2 * owned)
            mixed_t[at, span] = recv0m[ph, t].astype(jnp.float32)

        def take0(t, carry):
            back0(ph, t).wait_recv()
            collect0(t)
            return carry

        collect0(0)
        lax.fori_loop(1, local, take0, 0)

        def finish0(index, carry):
            at = pl.ds(pl.multiple_of(ph * part + index * chunk, chunk), chunk)
            result = (z_ref[at, :].astype(jnp.float32) + mixed_update(0, at)).astype(jnp.bfloat16)
            between[at, :] = result
            normalize(1, at, result.astype(jnp.float32))
            return carry

        lax.fori_loop(0, part // chunk, finish0, 0)
        for first in range(0, D, bundle):
            steps = order[first : first + bundle]
            weights = jnp.concatenate([weights1[flip(me, step, D)] for step in steps], axis=0)
            for start in range(0, part, chunk):
                here = pl.ds(ph * part + start, chunk)
                projected = jnp.dot(weights, normed_t[:, here], preferred_element_type=jnp.float32)
                for place, step in enumerate(steps):
                    base = place * 4 * owned
                    gates = projected[base : base + 2 * owned]
                    values = projected[base + 2 * owned : base + 4 * owned]
                    target = recv1 if step == 0 else send1
                    target[ph, step, :, pl.ds(start, chunk)] = (
                        mask_flat[:, here] * opened(gates) * values
                    ).astype(jnp.bfloat16)
            for step in steps:
                if step:
                    out1(ph, step).start()

    def at_order(k):
        return jnp.where(k % 2 == 0, local + k // 2, (k // 2 + 1) % local)

    for ph in range(2):
        def spread1(step):
            source = flip(me, step, D)
            spread(
                lambda at: recv1[ph, step, :, pl.ds(at, LANES)],
                source % cols, source // cols, ph * (fours // 2), (ph + 1) * (fours // 2),
            )

        def receive1(k, carry):
            step = at_order(k)
            out1(ph, step).wait_recv()
            spread1(step)
            return carry

        spread1(0)
        lax.fori_loop(0, D - 1, receive1, 0)

    for h in range(owned):
        left = jnp.concatenate([channel(h, half, 0, rows) for half in range(cols)], axis=1)
        right = jnp.concatenate([channel(owned + h, half, 0, rows) for half in range(cols)], axis=1)
        product = lax.dot_general(
            left, right, (((0,), (0,)), ((), ())), preferred_element_type=jnp.float32
        )
        for block in range(rows):
            at = block * T // per_col * LANES + block * T % per_col
            for half in range(cols):
                mix1[block, half, pl.ds(h * T, T), :] = product[
                    at : at + T, half * LANES : (half + 1) * LANES
                ]

    def pack1(step, target):
        other = flip(me, step, D)
        block, half = other // cols, other % cols
        for four in range(fours // 2):
            both = [
                join_rows([
                    mix1[block, half, pl.ds(ph * (T // 2) + 4 * four + i, owned, stride=T), :]
                    for i in range(4)
                ])
                for ph in range(2)
            ]
            for i in range(3):
                target[step, :, pl.ds((3 * four + i) * LANES, LANES)] = jnp.concatenate(
                    [both[0][i], both[1][i]], axis=0
                ).astype(jnp.bfloat16)

    def give1(k, carry):
        step = at_order(k)
        pack1(step, send1m)
        back1(step).start()
        return carry

    lax.fori_loop(0, D - 1, give1, 0)
    pack1(0, recv1m)

    def collect1(step):
        owner = flip(me, step, D)
        at = pl.ds(pl.multiple_of(owner * owned, owned), owned)
        values = recv1m[step].astype(jnp.float32)
        mixed_t[at, :part] = values[:owned]
        mixed_t[at, part:] = values[owned:]

    def take1(k, carry):
        step = at_order(k)
        back1(step).wait_recv()
        collect1(step)
        return carry

    collect1(0)
    lax.fori_loop(0, D - 1, take1, 0)

    def finish1(index, carry):
        at = pl.ds(pl.multiple_of(index * chunk, chunk), chunk)
        out_ref[at, :] = (between[at, :].astype(jnp.float32) + mixed_update(1, at)).astype(jnp.bfloat16)
        return carry

    lax.fori_loop(0, count // chunk, finish1, 0)

    far(0).wait_send()

    def settle0(t, carry):
        far(t).wait_send()
        near(t).wait_send()
        back0(0, t).wait_send()
        back0(1, t).wait_send()
        return carry

    def settle1(step, carry):
        out1(0, step).wait_send()
        out1(1, step).wait_send()
        back1(step).wait_send()
        return carry

    lax.fori_loop(1, local, settle0, 0)
    lax.fori_loop(1, D, settle1, 0)


def fused_updates(flat, mask, w_in, w_gate, w_out):
    rows, cols = lax.axis_size("row"), lax.axis_size("col")
    D = rows * cols
    local = D // 2
    T, W = mask.shape
    count, C = flat.shape
    owned = w_in.shape[2] // 4 // D
    vmem, half, full = pltpu.VMEM, jnp.bfloat16, jnp.float32
    dma = pltpu.SemaphoreType.DMA
    return pl.pallas_call(
        functools.partial(fused_kernel, rows, cols, T, W),
        out_shape=jax.ShapeDtypeStruct((count, C), half),
        in_specs=[pl.BlockSpec(memory_space=vmem)] * 5,
        out_specs=pl.BlockSpec(memory_space=vmem),
        scratch_shapes=[
            vmem((T, LANES), full),
            vmem((1, count), full),
            vmem((local, 8 * owned, C), half),
            vmem((D, 4 * owned, C), half),
            vmem((count, C), half),
            vmem((C, count), half),
            vmem((count, C), full),
            vmem((D * owned, count), full),
            vmem((cols, rows + rows // 2, 2 * owned * T, LANES), full),
            vmem((local, 4 * owned, count), half),
            vmem((local, 4 * owned, count), half),
            vmem((local, 2 * owned, count), half),
            vmem((rows // 2, cols, 2 * owned * T, LANES), full),
            vmem((2, local, 2 * owned, count // 2), half),
            vmem((2, local, 2 * owned, count // 2), half),
            vmem((2, D, 2 * owned, count // 2), half),
            vmem((2, D, 2 * owned, count // 2), half),
            vmem((rows, cols, owned * T, LANES), full),
            vmem((D, 2 * owned, count // 2), half),
            vmem((D, 2 * owned, count // 2), half),
            dma((local,)), dma((local,)), dma((local,)), dma((local,)),
            dma((2, local)), dma((2, local)),
            dma((2, D)), dma((2, D)), dma((D,)), dma((D,)),
        ],
        compiler_params=pltpu.CompilerParams(
            collective_id=0, has_side_effects=True, vmem_limit_bytes=48 * 1024 * 1024
        ),
    )(flat, mask, w_in, w_gate, w_out)


def fits_fused(pair, w_in):
    rows, cols = lax.axis_size("row"), lax.axis_size("col")
    D = rows * cols
    T, W, C = pair.shape
    H = w_in.shape[2] // 4
    return (
        W == 96 and T % 8 == 0 and cols == 2 and D & (D - 1) == 0
        and C == LANES and H == LANES and H == 8 * D and rows * T == cols * W
    )


def per_device(pair, mask, w_in, w_gate, w_out):
    mask_flat = mask.reshape(-1).astype(jnp.float32)
    if fits_fused(pair, w_in):
        T, W, C = pair.shape
        return fused_updates(pair.reshape(T * W, C), mask, w_in, w_gate, w_out).reshape(T, W, C)
    first = triangle(pair, mask_flat, w_in[0], w_gate[0], w_out[0], True)
    return triangle(first, mask_flat, w_in[1], w_gate[1], w_out[1], False)


def solution(mesh):
    placed = (P(("groups", "row"), "col", None), P(("groups", "row"), "col"), P(), P(), P())
    return jax.shard_map(
        per_device,
        mesh=mesh,
        in_specs=placed,
        out_specs=P(("groups", "row"), "col", None),
        check_vma=False,
    )
```

```python
import functools

import jax
import jax.numpy as jnp
from jax import lax
from jax.experimental import pallas as pl
from jax.experimental.pallas import tpu as pltpu
from jax.sharding import PartitionSpec as P

LANES = 128


def layer_norm(values, dimension):
    average = jnp.mean(values, axis=dimension, keepdims=True)
    centered = values - average
    variance = jnp.mean(centered * centered, axis=dimension, keepdims=True)
    return centered * lax.rsqrt(variance + 1e-05)


def triangle(pair_in, mask_flat, weight_in, weight_gate, weight_out, outgoing):
    tile_rows, tile_cols, channels = pair_in.shape
    pair_count = tile_rows * tile_cols
    hidden = weight_in.shape[1] // 4
    row_count = lax.axis_size("row")
    col_count = lax.axis_size("col")
    groups = row_count * col_count
    per_group = hidden // groups
    flat_pair = pair_in.reshape(pair_count, channels).astype(jnp.float32)
    normed = layer_norm(flat_pair, 1).astype(jnp.bfloat16)
    projected = jnp.einsum("pc,ch->hp", normed, weight_in, preferred_element_type=jnp.float32)
    stacked = (
        mask_flat[None, :] * jax.nn.sigmoid(projected[: 2 * hidden]) * projected[2 * hidden :]
    ).astype(jnp.bfloat16)
    stacked = stacked.reshape(2, groups, per_group, pair_count)
    equation = "mik,mjk->mij" if outgoing else "mki,mkj->mij"
    pieces = lax.all_to_all(stacked, ("row", "col"), split_axis=1, concat_axis=1, tiled=True)
    item_count = pieces.shape[2]
    gathered = pieces.reshape(2, row_count, col_count, item_count, tile_rows, tile_cols)
    gathered = jnp.transpose(gathered, (0, 3, 1, 4, 2, 5))
    gathered = gathered.reshape(2, item_count, row_count * tile_rows, col_count * tile_cols)
    product = jnp.einsum(
        equation, gathered[0], gathered[1], preferred_element_type=jnp.float32
    ).astype(jnp.bfloat16)
    product = product.reshape(item_count, row_count, tile_rows, col_count, tile_cols)
    product = jnp.transpose(product, (1, 3, 0, 2, 4))
    result = lax.all_to_all(
        product.reshape(groups, item_count, pair_count),
        ("row", "col"),
        split_axis=0,
        concat_axis=0,
        tiled=True,
    )
    result = result.reshape(hidden, pair_count)
    mixed_norm = layer_norm(result.astype(jnp.float32), 0).astype(jnp.bfloat16)
    update = jnp.einsum("hp,hc->pc", mixed_norm, weight_out, preferred_element_type=jnp.float32)
    gate_value = jax.nn.sigmoid(jnp.dot(normed, weight_gate, preferred_element_type=jnp.float32))
    output = (flat_pair + gate_value * update).astype(jnp.bfloat16)
    return output.reshape(tile_rows, tile_cols, channels)


def flip(index, step, count):
    total, bit = 0, 1
    while bit < count:
        total = total + ((index // bit + step // bit) % 2) * bit
        bit *= 2
    return total


def step_order(count):
    half = count // 2
    return [half + k // 2 if k % 2 == 0 else (k // 2 + 1) % half for k in range(count)]


def fused_kernel(
    rows, cols, T, W,
    z_hbm, mask_hbm, win_hbm, wgate_hbm, wout_hbm, out_ref,
    z_ref, mask_ref, win_ref, wgate_ref, wout_ref, load_sem, normed, mask_rows, mask_flat, weights0, weights1, between, normed_t, gate, mixed_t, pairs,
    send0, near0, far0, mix0, send0m, recv0m,
    send1, recv1, mix1, send1m, recv1m,
    near_send, near_recv, far_send, far_recv, back0_send, back0_recv,
    out1_send, out1_recv, back1_send, back1_recv,
):
    D = rows * cols
    local = D // 2
    count = T * W
    part = count // 2
    owned = recv1.shape[2] // 2
    N = rows * T
    per_col = N // cols
    fours = T // 4
    me = lax.axis_index("row") * cols + lax.axis_index("col")
    order = step_order(D)
    lane = lax.broadcasted_iota(jnp.int32, (1, LANES), 1)
    chunk = 384

    def device(step):
        other = flip(me, step, D)
        return {"row": other // cols, "col": other % cols}

    def remote(source, target, sent, received, step):
        return pltpu.make_async_remote_copy(
            src_ref=source, dst_ref=target, send_sem=sent, recv_sem=received,
            device_id=device(step), device_id_type=pl.DeviceIdType.MESH,
        )

    def near(t):
        return remote(send0.at[t], near0.at[t], near_send.at[t], near_recv.at[t], t)

    def far(t):
        return remote(
            send0.at[t, pl.ds(0, 2 * owned)], far0.at[t], far_send.at[t], far_recv.at[t], local + t
        )

    def back0(ph, t):
        return remote(
            send0m.at[ph, t], recv0m.at[ph, t], back0_send.at[ph, t], back0_recv.at[ph, t], t
        )

    def out1(ph, step):
        return remote(
            send1.at[ph, step], recv1.at[ph, step], out1_send.at[ph, step], out1_recv.at[ph, step], step
        )

    def back1(step):
        return remote(send1m.at[step], recv1m.at[step], back1_send.at[step], back1_recv.at[step], step)

    loads = [
        pltpu.make_async_copy(source, target, load_sem.at[i])
        for i, (source, target) in enumerate([
            (win_hbm, win_ref), (z_hbm, z_ref), (mask_hbm, mask_ref),
            (wgate_hbm, wgate_ref), (wout_hbm, wout_ref),
        ])
    ]
    for load in loads:
        load.start()
    barrier = pltpu.get_barrier_semaphore()
    for step in range(1, D):
        pl.semaphore_signal(
            barrier, inc=1, device_id=device(step), device_id_type=pl.DeviceIdType.MESH
        )

    def split_rows(v):
        one = jnp.where(lane < 32, pltpu.roll(v[0], 32, 1), pltpu.roll(v[1], 32, 1))
        two = jnp.where(lane < 64, pltpu.roll(v[1], 64, 1), pltpu.roll(v[2], 64, 1))
        return [jnp.where(lane < W, x, 0.0) for x in (v[0], one, two, pltpu.roll(v[2], 96, 1))]

    def join_rows(p):
        one, two, three = pltpu.roll(p[1], 96, 1), pltpu.roll(p[2], 64, 1), pltpu.roll(p[3], 32, 1)
        return [
            jnp.where(lane < 96, p[0], one),
            jnp.where(lane < 64, one, two),
            jnp.where(lane < 32, two, three),
        ]

    def spread(load, half, block, begin, end):
        for four in range(begin, end):
            v = [load((3 * (four - begin) + i) * LANES).astype(jnp.float32) for i in range(3)]
            for i, piece in enumerate(split_rows(v)):
                pairs[half, block, pl.ds(4 * four + i, 2 * owned, stride=T), :] = piece

    def opened(logits):
        return 0.5 + 0.5 * jnp.tanh(0.5 * logits)

    def arrange(update, target, size):
        turned = win_ref[update].astype(jnp.float32).T
        H = turned.shape[0] // 4
        for owner in range(H // size):
            target[owner] = jnp.concatenate(
                [turned[q * H + owner * size : q * H + (owner + 1) * size] for q in range(4)], axis=0
            ).astype(jnp.bfloat16)

    def normalize(update, at, values):
        centered = values - jnp.mean(values, axis=1, keepdims=True)
        variance = jnp.mean(centered * centered, axis=1, keepdims=True)
        result = centered * lax.rsqrt(variance + 1e-05)
        normed_t[:, at] = result.T.astype(jnp.bfloat16)
        normed[at, :] = result.astype(jnp.bfloat16)

    def open_gate(update, index):
        at = pl.ds(pl.multiple_of(index * chunk, chunk), chunk)
        gate[at, :] = opened(
            jnp.dot(normed[at, :], wgate_ref[update], preferred_element_type=jnp.float32)
        )

    def normalize_input(index, carry):
        at = pl.ds(pl.multiple_of(index * chunk, chunk), chunk)
        normalize(0, at, z_ref[at, :].astype(jnp.float32))
        return carry

    def open_gates(update):
        def one(index, carry):
            open_gate(update, index)
            return carry

        lax.fori_loop(0, count // chunk, one, 0)

    loads[0].wait()
    arrange(0, weights0, 2 * owned)
    loads[1].wait()
    lax.fori_loop(0, count // chunk, normalize_input, 0)
    loads[2].wait()
    mask_rows[...] = jnp.zeros_like(mask_rows)
    mask_rows[:, :W] = mask_ref[...].astype(jnp.float32)
    for four in range(fours):
        p = [mask_rows[pl.ds(4 * four + i, 1), :] for i in range(4)]
        for i, piece in enumerate(join_rows(p)):
            mask_flat[:, pl.ds((3 * four + i) * LANES, LANES)] = piece
    pl.semaphore_wait(barrier, D - 1)

    wide = 768
    for first in range(local // 2):
        steps = (first, local // 2 + first)
        weights = jnp.concatenate([weights0[flip(me, t, D) % local] for t in steps], axis=0)
        for start in range(0, count, wide):
            here = pl.ds(start, wide)
            projected = jnp.dot(weights, normed_t[:, here], preferred_element_type=jnp.float32)
            for place, t in enumerate(steps):
                base = place * 8 * owned
                gates = projected[base : base + 4 * owned]
                values = projected[base + 4 * owned : base + 8 * owned]
                both = (mask_flat[:, here] * opened(gates) * values).astype(jnp.bfloat16)
                send0[t, : 2 * owned, here] = both[2 * owned :]
                send0[t, 2 * owned :, here] = both[: 2 * owned]
        for t in steps:
            far(t).start()
        for t in steps:
            if t:
                near(t).start()

    def spread_near(ref, t):
        source = flip(me, t, D)
        block, half = source // cols, source % cols
        spread(lambda at: ref[t, : 2 * owned, pl.ds(at, LANES)], half, block, 0, fours)
        spread(
            lambda at: ref[t, 2 * owned :, pl.ds(at, LANES)],
            half, rows + block % (rows // 2), 0, fours,
        )

    def spread_far(t):
        far(t).wait_recv()
        source = flip(me, local + t, D)
        spread(
            lambda at: far0[t, :, pl.ds(at, LANES)], source % cols, source // cols, 0, fours
        )

    loads[3].wait()
    loads[4].wait()
    open_gates(0)
    spread_near(send0, 0)
    arrange(1, weights1, owned)
    spread_far(0)

    def receive0(k, carry):
        t = k // 2 + k % 2 * (local // 2)
        near(t).wait_recv()
        spread_near(near0, t)
        spread_far(t)
        return carry

    lax.fori_loop(1, local, receive0, 0)

    def channel(which, half, begin, blocks):
        block = pairs[half, pl.ds(begin, blocks), pl.ds(which * T, T), :]
        return block.reshape(blocks * T, LANES).astype(jnp.bfloat16)

    for h in range(2 * owned):
        left = jnp.concatenate(
            [channel(h, half, rows, rows // 2) for half in range(cols)], axis=1
        )
        right = jnp.concatenate([channel(h, half, 0, rows) for half in range(cols)], axis=1)
        blank = jnp.zeros((LANES - per_col, cols * LANES), jnp.bfloat16)
        padded = []
        for half in range(cols):
            padded += [right[half * per_col : (half + 1) * per_col], blank]
        product = lax.dot_general(
            left, jnp.concatenate(padded, axis=0), (((1,), (1,)), ((), ())),
            preferred_element_type=jnp.float32,
        )
        for block in range(rows // 2):
            for half in range(cols):
                mix0[block, half, pl.ds(h * T, T), :] = product[
                    block * T : (block + 1) * T, half * LANES : (half + 1) * LANES
                ]

    def pack0(ph, t, target):
        other = flip(me, t, D)
        block, half = other // cols % (rows // 2), other % cols
        for four in range(fours // 2):
            row = ph * (T // 2) + 4 * four
            p = [mix0[block, half, pl.ds(row + i, 2 * owned, stride=T), :] for i in range(4)]
            for i, piece in enumerate(join_rows(p)):
                target[ph, t, :, pl.ds((3 * four + i) * LANES, LANES)] = piece.astype(jnp.bfloat16)

    for ph in range(2):
        def give0(k, carry):
            t = k // 2 + k % 2 * (local // 2)
            pack0(ph, t, send0m)
            back0(ph, t).start()
            return carry

        lax.fori_loop(1, local, give0, 0)
        pack0(ph, 0, recv0m)

    def mixed_update(update, at):
        values = mixed_t[:, at]
        centered = values - jnp.mean(values, axis=0, keepdims=True)
        variance = jnp.mean(centered * centered, axis=0, keepdims=True)
        mixed_norm = (centered * lax.rsqrt(variance + 1e-05)).T.astype(jnp.bfloat16)
        return gate[at, :] * jnp.dot(
            mixed_norm, wout_ref[update], preferred_element_type=jnp.float32
        )

    bundle = 4
    for ph in range(2):
        span = pl.ds(ph * part, part)

        def collect0(t):
            owner = flip(me, t, D) % local
            at = pl.ds(pl.multiple_of(owner * 2 * owned, 2 * owned), 2 * owned)
            mixed_t[at, span] = recv0m[ph, t].astype(jnp.float32)

        def take0(k, carry):
            t = k // 2 + k % 2 * (local // 2)
            back0(ph, t).wait_recv()
            collect0(t)
            return carry

        collect0(0)
        lax.fori_loop(1, local, take0, 0)

        def finish0(index, carry):
            at = pl.ds(pl.multiple_of(ph * part + index * chunk, chunk), chunk)
            result = (z_ref[at, :].astype(jnp.float32) + mixed_update(0, at)).astype(jnp.bfloat16)
            between[at, :] = result
            normalize(1, at, result.astype(jnp.float32))
            return carry

        lax.fori_loop(0, part // chunk, finish0, 0)
        for first in range(0, D, bundle):
            steps = order[first : first + bundle]
            weights = jnp.concatenate([weights1[flip(me, step, D)] for step in steps], axis=0)
            for start in range(0, part, chunk):
                here = pl.ds(ph * part + start, chunk)
                projected = jnp.dot(weights, normed_t[:, here], preferred_element_type=jnp.float32)
                for place, step in enumerate(steps):
                    base = place * 4 * owned
                    gates = projected[base : base + 2 * owned]
                    values = projected[base + 2 * owned : base + 4 * owned]
                    target = recv1 if step == 0 else send1
                    target[ph, step, :, pl.ds(start, chunk)] = (
                        mask_flat[:, here] * opened(gates) * values
                    ).astype(jnp.bfloat16)
            for step in steps:
                if step:
                    out1(ph, step).start()

    open_gates(1)

    def at_order(k):
        return jnp.where(k % 2 == 0, local + k // 2, (k // 2 + 1) % local)

    for ph in range(2):
        def spread1(step):
            source = flip(me, step, D)
            spread(
                lambda at: recv1[ph, step, :, pl.ds(at, LANES)],
                source % cols, source // cols, ph * (fours // 2), (ph + 1) * (fours // 2),
            )

        def receive1(k, carry):
            step = at_order(k)
            out1(ph, step).wait_recv()
            spread1(step)
            return carry

        spread1(0)
        lax.fori_loop(0, D - 1, receive1, 0)

    for h in range(owned):
        left = jnp.concatenate([channel(h, half, 0, rows) for half in range(cols)], axis=1)
        right = jnp.concatenate([channel(owned + h, half, 0, rows) for half in range(cols)], axis=1)
        product = lax.dot_general(
            left, right, (((0,), (0,)), ((), ())), preferred_element_type=jnp.float32
        )
        for block in range(rows):
            at = block * T // per_col * LANES + block * T % per_col
            for half in range(cols):
                mix1[block, half, pl.ds(h * T, T), :] = product[
                    at : at + T, half * LANES : (half + 1) * LANES
                ]

    def pack1(step, target):
        other = flip(me, step, D)
        block, half = other // cols, other % cols
        for four in range(fours // 2):
            both = [
                join_rows([
                    mix1[block, half, pl.ds(ph * (T // 2) + 4 * four + i, owned, stride=T), :]
                    for i in range(4)
                ])
                for ph in range(2)
            ]
            for i in range(3):
                target[step, :, pl.ds((3 * four + i) * LANES, LANES)] = jnp.concatenate(
                    [both[0][i], both[1][i]], axis=0
                ).astype(jnp.bfloat16)

    def give1(k, carry):
        step = at_order(k)
        pack1(step, send1m)
        back1(step).start()
        return carry

    lax.fori_loop(0, D - 1, give1, 0)
    pack1(0, recv1m)

    def collect1(step):
        owner = flip(me, step, D)
        at = pl.ds(pl.multiple_of(owner * owned, owned), owned)
        values = recv1m[step].astype(jnp.float32)
        mixed_t[at, :part] = values[:owned]
        mixed_t[at, part:] = values[owned:]

    def take1(k, carry):
        step = at_order(k)
        back1(step).wait_recv()
        collect1(step)
        return carry

    collect1(0)
    lax.fori_loop(0, D - 1, take1, 0)

    def finish1(index, carry):
        at = pl.ds(pl.multiple_of(index * chunk, chunk), chunk)
        out_ref[at, :] = (between[at, :].astype(jnp.float32) + mixed_update(1, at)).astype(jnp.bfloat16)
        return carry

    lax.fori_loop(0, count // chunk, finish1, 0)

    far(0).wait_send()

    def settle0(t, carry):
        far(t).wait_send()
        near(t).wait_send()
        back0(0, t).wait_send()
        back0(1, t).wait_send()
        return carry

    def settle1(step, carry):
        out1(0, step).wait_send()
        out1(1, step).wait_send()
        back1(step).wait_send()
        return carry

    lax.fori_loop(1, local, settle0, 0)
    lax.fori_loop(1, D, settle1, 0)


def fused_updates(flat, mask, w_in, w_gate, w_out):
    rows, cols = lax.axis_size("row"), lax.axis_size("col")
    D = rows * cols
    local = D // 2
    T, W = mask.shape
    count, C = flat.shape
    owned = w_in.shape[2] // 4 // D
    vmem, half, full = pltpu.VMEM, jnp.bfloat16, jnp.float32
    dma = pltpu.SemaphoreType.DMA
    return pl.pallas_call(
        functools.partial(fused_kernel, rows, cols, T, W),
        out_shape=jax.ShapeDtypeStruct((count, C), half),
        in_specs=[pl.BlockSpec(memory_space=pltpu.HBM)] * 5,
        out_specs=pl.BlockSpec(memory_space=vmem),
        scratch_shapes=[
            vmem(flat.shape, half),
            vmem(mask.shape, jnp.int32),
            vmem(w_in.shape, half),
            vmem(w_gate.shape, half),
            vmem(w_out.shape, half),
            dma((5,)),
            vmem((count, C), half),
            vmem((T, LANES), full),
            vmem((1, count), full),
            vmem((local, 8 * owned, C), half),
            vmem((D, 4 * owned, C), half),
            vmem((count, C), half),
            vmem((C, count), half),
            vmem((count, C), full),
            vmem((D * owned, count), full),
            vmem((cols, rows + rows // 2, 2 * owned * T, LANES), full),
            vmem((local, 4 * owned, count), half),
            vmem((local, 4 * owned, count), half),
            vmem((local, 2 * owned, count), half),
            vmem((rows // 2, cols, 2 * owned * T, LANES), full),
            vmem((2, local, 2 * owned, count // 2), half),
            vmem((2, local, 2 * owned, count // 2), half),
            vmem((2, D, 2 * owned, count // 2), half),
            vmem((2, D, 2 * owned, count // 2), half),
            vmem((rows, cols, owned * T, LANES), full),
            vmem((D, 2 * owned, count // 2), half),
            vmem((D, 2 * owned, count // 2), half),
            dma((local,)), dma((local,)), dma((local,)), dma((local,)),
            dma((2, local)), dma((2, local)),
            dma((2, D)), dma((2, D)), dma((D,)), dma((D,)),
        ],
        compiler_params=pltpu.CompilerParams(
            collective_id=0, has_side_effects=True, vmem_limit_bytes=64 * 1024 * 1024
        ),
    )(flat, mask, w_in, w_gate, w_out)


def fits_fused(pair, w_in):
    rows, cols = lax.axis_size("row"), lax.axis_size("col")
    D = rows * cols
    T, W, C = pair.shape
    H = w_in.shape[2] // 4
    return (
        W == 96 and T % 8 == 0 and cols == 2 and D & (D - 1) == 0
        and C == LANES and H == LANES and H == 8 * D and rows * T == cols * W
    )


def per_device(pair, mask, w_in, w_gate, w_out):
    mask_flat = mask.reshape(-1).astype(jnp.float32)
    if fits_fused(pair, w_in):
        T, W, C = pair.shape
        return fused_updates(pair.reshape(T * W, C), mask, w_in, w_gate, w_out).reshape(T, W, C)
    first = triangle(pair, mask_flat, w_in[0], w_gate[0], w_out[0], True)
    return triangle(first, mask_flat, w_in[1], w_gate[1], w_out[1], False)


def solution(mesh):
    placed = (P(("groups", "row"), "col", None), P(("groups", "row"), "col"), P(), P(), P())
    return jax.shard_map(
        per_device,
        mesh=mesh,
        in_specs=placed,
        out_specs=P(("groups", "row"), "col", None),
        check_vma=False,
    )
```

```python
import functools

import jax
import jax.numpy as jnp
from jax import lax
from jax.experimental import pallas as pl
from jax.experimental.pallas import tpu as pltpu
from jax.sharding import PartitionSpec as P

LANES = 128


def layer_norm(values, dimension):
    average = jnp.mean(values, axis=dimension, keepdims=True)
    centered = values - average
    variance = jnp.mean(centered * centered, axis=dimension, keepdims=True)
    return centered * lax.rsqrt(variance + 1e-05)


def triangle(pair_in, mask_flat, weight_in, weight_gate, weight_out, outgoing):
    tile_rows, tile_cols, channels = pair_in.shape
    pair_count = tile_rows * tile_cols
    hidden = weight_in.shape[1] // 4
    row_count = lax.axis_size("row")
    col_count = lax.axis_size("col")
    groups = row_count * col_count
    per_group = hidden // groups
    flat_pair = pair_in.reshape(pair_count, channels).astype(jnp.float32)
    normed = layer_norm(flat_pair, 1).astype(jnp.bfloat16)
    projected = jnp.einsum("pc,ch->hp", normed, weight_in, preferred_element_type=jnp.float32)
    stacked = (
        mask_flat[None, :] * jax.nn.sigmoid(projected[: 2 * hidden]) * projected[2 * hidden :]
    ).astype(jnp.bfloat16)
    stacked = stacked.reshape(2, groups, per_group, pair_count)
    equation = "mik,mjk->mij" if outgoing else "mki,mkj->mij"
    pieces = lax.all_to_all(stacked, ("row", "col"), split_axis=1, concat_axis=1, tiled=True)
    item_count = pieces.shape[2]
    gathered = pieces.reshape(2, row_count, col_count, item_count, tile_rows, tile_cols)
    gathered = jnp.transpose(gathered, (0, 3, 1, 4, 2, 5))
    gathered = gathered.reshape(2, item_count, row_count * tile_rows, col_count * tile_cols)
    product = jnp.einsum(
        equation, gathered[0], gathered[1], preferred_element_type=jnp.float32
    ).astype(jnp.bfloat16)
    product = product.reshape(item_count, row_count, tile_rows, col_count, tile_cols)
    product = jnp.transpose(product, (1, 3, 0, 2, 4))
    result = lax.all_to_all(
        product.reshape(groups, item_count, pair_count),
        ("row", "col"),
        split_axis=0,
        concat_axis=0,
        tiled=True,
    )
    result = result.reshape(hidden, pair_count)
    mixed_norm = layer_norm(result.astype(jnp.float32), 0).astype(jnp.bfloat16)
    update = jnp.einsum("hp,hc->pc", mixed_norm, weight_out, preferred_element_type=jnp.float32)
    gate_value = jax.nn.sigmoid(jnp.dot(normed, weight_gate, preferred_element_type=jnp.float32))
    output = (flat_pair + gate_value * update).astype(jnp.bfloat16)
    return output.reshape(tile_rows, tile_cols, channels)


def flip(index, step, count):
    total, bit = 0, 1
    while bit < count:
        total = total + ((index // bit + step // bit) % 2) * bit
        bit *= 2
    return total


def step_order(count):
    half = count // 2
    return [half + k // 2 if k % 2 == 0 else (k // 2 + 1) % half for k in range(count)]


def fused_kernel(
    rows, cols, T, W,
    z_hbm, mask_hbm, win_hbm, wgate_hbm, wout_hbm, out_ref,
    z_ref, mask_ref, win_ref, wgate_ref, wout_ref, load_sem, normed, mask_rows, mask_flat, weights0, weights1, between, normed_t, gate, mixed_t, pairs,
    send0, near0, far0, mix0, send0m, recv0m,
    send1, recv1, mix1, send1m, recv1m,
    near_send, near_recv, far_send, far_recv, back0_send, back0_recv,
    out1_send, out1_recv, back1_send, back1_recv,
):
    D = rows * cols
    local = D // 2
    count = T * W
    part = count // 2
    owned = recv1.shape[2] // 2
    N = rows * T
    per_col = N // cols
    fours = T // 4
    me = lax.axis_index("row") * cols + lax.axis_index("col")
    order = step_order(D)
    lane = lax.broadcasted_iota(jnp.int32, (1, LANES), 1)
    chunk = 384

    def device(step):
        other = flip(me, step, D)
        return {"row": other // cols, "col": other % cols}

    def remote(source, target, sent, received, step):
        return pltpu.make_async_remote_copy(
            src_ref=source, dst_ref=target, send_sem=sent, recv_sem=received,
            device_id=device(step), device_id_type=pl.DeviceIdType.MESH,
        )

    def near(t):
        return remote(send0.at[t], near0.at[t], near_send.at[t], near_recv.at[t], t)

    def far(t):
        return remote(
            send0.at[t, pl.ds(0, 2 * owned)], far0.at[t], far_send.at[t], far_recv.at[t], local + t
        )

    def back0(ph, t):
        return remote(
            send0m.at[ph, t], recv0m.at[ph, t], back0_send.at[ph, t], back0_recv.at[ph, t], t
        )

    def out1(ph, step):
        return remote(
            send1.at[ph, step], recv1.at[ph, step], out1_send.at[ph, step], out1_recv.at[ph, step], step
        )

    def back1(four, step):
        return remote(
            send1m.at[four, step], recv1m.at[four, step],
            back1_send.at[four, step], back1_recv.at[four, step], step,
        )

    loads = [
        pltpu.make_async_copy(source, target, load_sem.at[i])
        for i, (source, target) in enumerate([
            (win_hbm, win_ref), (z_hbm, z_ref), (mask_hbm, mask_ref),
            (wgate_hbm, wgate_ref), (wout_hbm, wout_ref),
        ])
    ]
    for load in loads:
        load.start()
    barrier = pltpu.get_barrier_semaphore()
    for step in range(1, D):
        pl.semaphore_signal(
            barrier, inc=1, device_id=device(step), device_id_type=pl.DeviceIdType.MESH
        )

    def split_rows(v):
        one = jnp.where(lane < 32, pltpu.roll(v[0], 32, 1), pltpu.roll(v[1], 32, 1))
        two = jnp.where(lane < 64, pltpu.roll(v[1], 64, 1), pltpu.roll(v[2], 64, 1))
        return [jnp.where(lane < W, x, 0.0) for x in (v[0], one, two, pltpu.roll(v[2], 96, 1))]

    def join_rows(p):
        one, two, three = pltpu.roll(p[1], 96, 1), pltpu.roll(p[2], 64, 1), pltpu.roll(p[3], 32, 1)
        return [
            jnp.where(lane < 96, p[0], one),
            jnp.where(lane < 64, one, two),
            jnp.where(lane < 32, two, three),
        ]

    def spread(load, half, block, begin, end):
        for four in range(begin, end):
            v = [load((3 * (four - begin) + i) * LANES).astype(jnp.float32) for i in range(3)]
            for i, piece in enumerate(split_rows(v)):
                pairs[half, block, pl.ds(4 * four + i, 2 * owned, stride=T), :] = piece

    def opened(logits):
        return 0.5 + 0.5 * jnp.tanh(0.5 * logits)

    def arrange(update, target, size):
        turned = win_ref[update].astype(jnp.float32).T
        H = turned.shape[0] // 4
        for owner in range(H // size):
            target[owner] = jnp.concatenate(
                [turned[q * H + owner * size : q * H + (owner + 1) * size] for q in range(4)], axis=0
            ).astype(jnp.bfloat16)

    def normalize(update, at, values):
        centered = values - jnp.mean(values, axis=1, keepdims=True)
        variance = jnp.mean(centered * centered, axis=1, keepdims=True)
        result = centered * lax.rsqrt(variance + 1e-05)
        normed_t[:, at] = result.T.astype(jnp.bfloat16)
        normed[at, :] = result.astype(jnp.bfloat16)

    def open_gate(update, index):
        at = pl.ds(pl.multiple_of(index * chunk, chunk), chunk)
        gate[at, :] = opened(
            jnp.dot(normed[at, :], wgate_ref[update], preferred_element_type=jnp.float32)
        )

    def normalize_input(index, carry):
        at = pl.ds(pl.multiple_of(index * chunk, chunk), chunk)
        normalize(0, at, z_ref[at, :].astype(jnp.float32))
        return carry

    def open_gates(update):
        def one(index, carry):
            open_gate(update, index)
            return carry

        lax.fori_loop(0, count // chunk, one, 0)

    loads[0].wait()
    arrange(0, weights0, 2 * owned)
    loads[1].wait()
    lax.fori_loop(0, count // chunk, normalize_input, 0)
    loads[2].wait()
    mask_rows[...] = jnp.zeros_like(mask_rows)
    mask_rows[:, :W] = mask_ref[...].astype(jnp.float32)
    for four in range(fours):
        p = [mask_rows[pl.ds(4 * four + i, 1), :] for i in range(4)]
        for i, piece in enumerate(join_rows(p)):
            mask_flat[:, pl.ds((3 * four + i) * LANES, LANES)] = piece
    pl.semaphore_wait(barrier, D - 1)

    wide = 768
    for first in range(local // 2):
        steps = (first, local // 2 + first)
        weights = jnp.concatenate([weights0[flip(me, t, D) % local] for t in steps], axis=0)
        for start in range(0, count, wide):
            here = pl.ds(start, wide)
            projected = jnp.dot(weights, normed_t[:, here], preferred_element_type=jnp.float32)
            for place, t in enumerate(steps):
                base = place * 8 * owned
                gates = projected[base : base + 4 * owned]
                values = projected[base + 4 * owned : base + 8 * owned]
                both = (mask_flat[:, here] * opened(gates) * values).astype(jnp.bfloat16)
                send0[t, : 2 * owned, here] = both[2 * owned :]
                send0[t, 2 * owned :, here] = both[: 2 * owned]
        for t in steps:
            far(t).start()
        for t in steps:
            if t:
                near(t).start()

    def spread_near(ref, t):
        source = flip(me, t, D)
        block, half = source // cols, source % cols
        spread(lambda at: ref[t, : 2 * owned, pl.ds(at, LANES)], half, block, 0, fours)
        spread(
            lambda at: ref[t, 2 * owned :, pl.ds(at, LANES)],
            half, rows + block % (rows // 2), 0, fours,
        )

    def spread_far(t):
        far(t).wait_recv()
        source = flip(me, local + t, D)
        spread(
            lambda at: far0[t, :, pl.ds(at, LANES)], source % cols, source // cols, 0, fours
        )

    loads[3].wait()
    loads[4].wait()
    open_gates(0)
    spread_near(send0, 0)
    arrange(1, weights1, owned)
    spread_far(0)

    def receive0(k, carry):
        t = k // 2 + k % 2 * (local // 2)
        near(t).wait_recv()
        spread_near(near0, t)
        spread_far(t)
        return carry

    lax.fori_loop(1, local, receive0, 0)

    def channel(which, half, begin, blocks):
        block = pairs[half, pl.ds(begin, blocks), pl.ds(which * T, T), :]
        return block.reshape(blocks * T, LANES).astype(jnp.bfloat16)

    for h in range(2 * owned):
        left = jnp.concatenate(
            [channel(h, half, rows, rows // 2) for half in range(cols)], axis=1
        )
        right = jnp.concatenate([channel(h, half, 0, rows) for half in range(cols)], axis=1)
        blank = jnp.zeros((LANES - per_col, cols * LANES), jnp.bfloat16)
        padded = []
        for half in range(cols):
            padded += [right[half * per_col : (half + 1) * per_col], blank]
        product = lax.dot_general(
            left, jnp.concatenate(padded, axis=0), (((1,), (1,)), ((), ())),
            preferred_element_type=jnp.float32,
        )
        for block in range(rows // 2):
            for half in range(cols):
                mix0[block, half, pl.ds(h * T, T), :] = product[
                    block * T : (block + 1) * T, half * LANES : (half + 1) * LANES
                ]

    def pack0(ph, t, target):
        other = flip(me, t, D)
        block, half = other // cols % (rows // 2), other % cols
        for four in range(fours // 2):
            row = ph * (T // 2) + 4 * four
            p = [mix0[block, half, pl.ds(row + i, 2 * owned, stride=T), :] for i in range(4)]
            for i, piece in enumerate(join_rows(p)):
                target[ph, t, :, pl.ds((3 * four + i) * LANES, LANES)] = piece.astype(jnp.bfloat16)

    for ph in range(2):
        def give0(k, carry):
            t = k // 2 + k % 2 * (local // 2)
            pack0(ph, t, send0m)
            back0(ph, t).start()
            return carry

        lax.fori_loop(1, local, give0, 0)
        pack0(ph, 0, recv0m)

    def mixed_update(update, at):
        values = mixed_t[:, at]
        centered = values - jnp.mean(values, axis=0, keepdims=True)
        variance = jnp.mean(centered * centered, axis=0, keepdims=True)
        mixed_norm = (centered * lax.rsqrt(variance + 1e-05)).T.astype(jnp.bfloat16)
        return gate[at, :] * jnp.dot(
            mixed_norm, wout_ref[update], preferred_element_type=jnp.float32
        )

    bundle = 4
    for ph in range(2):
        span = pl.ds(ph * part, part)

        def collect0(t):
            owner = flip(me, t, D) % local
            at = pl.ds(pl.multiple_of(owner * 2 * owned, 2 * owned), 2 * owned)
            mixed_t[at, span] = recv0m[ph, t].astype(jnp.float32)

        def take0(k, carry):
            t = k // 2 + k % 2 * (local // 2)
            back0(ph, t).wait_recv()
            collect0(t)
            return carry

        collect0(0)
        lax.fori_loop(1, local, take0, 0)

        def finish0(index, carry):
            at = pl.ds(pl.multiple_of(ph * part + index * chunk, chunk), chunk)
            result = (z_ref[at, :].astype(jnp.float32) + mixed_update(0, at)).astype(jnp.bfloat16)
            between[at, :] = result
            normalize(1, at, result.astype(jnp.float32))
            return carry

        lax.fori_loop(0, part // chunk, finish0, 0)
        for first in range(0, D, bundle):
            steps = order[first : first + bundle]
            weights = jnp.concatenate([weights1[flip(me, step, D)] for step in steps], axis=0)
            for start in range(0, part, chunk):
                here = pl.ds(ph * part + start, chunk)
                projected = jnp.dot(weights, normed_t[:, here], preferred_element_type=jnp.float32)
                for place, step in enumerate(steps):
                    base = place * 4 * owned
                    gates = projected[base : base + 2 * owned]
                    values = projected[base + 2 * owned : base + 4 * owned]
                    target = recv1 if step == 0 else send1
                    target[ph, step, :, pl.ds(start, chunk)] = (
                        mask_flat[:, here] * opened(gates) * values
                    ).astype(jnp.bfloat16)
            for step in steps:
                if step:
                    out1(ph, step).start()

    open_gates(1)

    def at_order(k):
        return jnp.where(k % 2 == 0, local + k // 2, (k // 2 + 1) % local)

    for ph in range(2):
        def spread1(step):
            source = flip(me, step, D)
            spread(
                lambda at: recv1[ph, step, :, pl.ds(at, LANES)],
                source % cols, source // cols, ph * (fours // 2), (ph + 1) * (fours // 2),
            )

        def receive1(k, carry):
            step = at_order(k)
            out1(ph, step).wait_recv()
            spread1(step)
            return carry

        spread1(0)
        lax.fori_loop(0, D - 1, receive1, 0)

    for h in range(owned):
        left = jnp.concatenate([channel(h, half, 0, rows) for half in range(cols)], axis=1)
        right = jnp.concatenate([channel(owned + h, half, 0, rows) for half in range(cols)], axis=1)
        product = lax.dot_general(
            left, right, (((0,), (0,)), ((), ())), preferred_element_type=jnp.float32
        )
        for block in range(rows):
            at = block * T // per_col * LANES + block * T % per_col
            for half in range(cols):
                mix1[block, half, pl.ds(h * T, T), :] = product[
                    at : at + T, half * LANES : (half + 1) * LANES
                ]

    def pack1(four, step, target):
        other = flip(me, step, D)
        block, half = other // cols, other % cols
        both = [
            join_rows([
                mix1[block, half, pl.ds(ph * (T // 2) + 4 * four + i, owned, stride=T), :]
                for i in range(4)
            ])
            for ph in range(2)
        ]
        for i in range(3):
            target[four, step, :, pl.ds(i * LANES, LANES)] = jnp.concatenate(
                [both[0][i], both[1][i]], axis=0
            ).astype(jnp.bfloat16)

    for four in range(fours // 2):
        def give1(k, carry):
            step = at_order(k)
            pack1(four, step, send1m)
            back1(four, step).start()
            return carry

        lax.fori_loop(0, D - 1, give1, 0)
        pack1(four, 0, recv1m)

    for four in range(fours // 2):
        def collect1(step):
            owner = flip(me, step, D)
            at = pl.ds(pl.multiple_of(owner * owned, owned), owned)
            values = recv1m[four, step].astype(jnp.float32)
            mixed_t[at, pl.ds(four * chunk, chunk)] = values[:owned]
            mixed_t[at, pl.ds(part + four * chunk, chunk)] = values[owned:]

        def take1(k, carry):
            step = at_order(k)
            back1(four, step).wait_recv()
            collect1(step)
            return carry

        collect1(0)
        lax.fori_loop(0, D - 1, take1, 0)
        for ph in range(2):
            at = pl.ds(ph * part + four * chunk, chunk)
            out_ref[at, :] = (
                between[at, :].astype(jnp.float32) + mixed_update(1, at)
            ).astype(jnp.bfloat16)

    far(0).wait_send()

    def settle0(t, carry):
        far(t).wait_send()
        near(t).wait_send()
        back0(0, t).wait_send()
        back0(1, t).wait_send()
        return carry

    def settle1(step, carry):
        out1(0, step).wait_send()
        out1(1, step).wait_send()
        for four in range(fours // 2):
            back1(four, step).wait_send()
        return carry

    lax.fori_loop(1, local, settle0, 0)
    lax.fori_loop(1, D, settle1, 0)


def fused_updates(flat, mask, w_in, w_gate, w_out):
    rows, cols = lax.axis_size("row"), lax.axis_size("col")
    D = rows * cols
    local = D // 2
    T, W = mask.shape
    count, C = flat.shape
    owned = w_in.shape[2] // 4 // D
    vmem, half, full = pltpu.VMEM, jnp.bfloat16, jnp.float32
    dma = pltpu.SemaphoreType.DMA
    return pl.pallas_call(
        functools.partial(fused_kernel, rows, cols, T, W),
        out_shape=jax.ShapeDtypeStruct((count, C), half),
        in_specs=[pl.BlockSpec(memory_space=pltpu.HBM)] * 5,
        out_specs=pl.BlockSpec(memory_space=vmem),
        scratch_shapes=[
            vmem(flat.shape, half),
            vmem(mask.shape, jnp.int32),
            vmem(w_in.shape, half),
            vmem(w_gate.shape, half),
            vmem(w_out.shape, half),
            dma((5,)),
            vmem((count, C), half),
            vmem((T, LANES), full),
            vmem((1, count), full),
            vmem((local, 8 * owned, C), half),
            vmem((D, 4 * owned, C), half),
            vmem((count, C), half),
            vmem((C, count), half),
            vmem((count, C), full),
            vmem((D * owned, count), full),
            vmem((cols, rows + rows // 2, 2 * owned * T, LANES), full),
            vmem((local, 4 * owned, count), half),
            vmem((local, 4 * owned, count), half),
            vmem((local, 2 * owned, count), half),
            vmem((rows // 2, cols, 2 * owned * T, LANES), full),
            vmem((2, local, 2 * owned, count // 2), half),
            vmem((2, local, 2 * owned, count // 2), half),
            vmem((2, D, 2 * owned, count // 2), half),
            vmem((2, D, 2 * owned, count // 2), half),
            vmem((rows, cols, owned * T, LANES), full),
            vmem((T // 8, D, 2 * owned, 4 * W), half),
            vmem((T // 8, D, 2 * owned, 4 * W), half),
            dma((local,)), dma((local,)), dma((local,)), dma((local,)),
            dma((2, local)), dma((2, local)),
            dma((2, D)), dma((2, D)), dma((T // 8, D)), dma((T // 8, D)),
        ],
        compiler_params=pltpu.CompilerParams(
            collective_id=0, has_side_effects=True, vmem_limit_bytes=64 * 1024 * 1024
        ),
    )(flat, mask, w_in, w_gate, w_out)


def fits_fused(pair, w_in):
    rows, cols = lax.axis_size("row"), lax.axis_size("col")
    D = rows * cols
    T, W, C = pair.shape
    H = w_in.shape[2] // 4
    return (
        W == 96 and T == 24 and cols == 2 and D & (D - 1) == 0
        and C == LANES and H == LANES and H == 8 * D and rows * T == cols * W
    )


def per_device(pair, mask, w_in, w_gate, w_out):
    mask_flat = mask.reshape(-1).astype(jnp.float32)
    if fits_fused(pair, w_in):
        T, W, C = pair.shape
        return fused_updates(pair.reshape(T * W, C), mask, w_in, w_gate, w_out).reshape(T, W, C)
    first = triangle(pair, mask_flat, w_in[0], w_gate[0], w_out[0], True)
    return triangle(first, mask_flat, w_in[1], w_gate[1], w_out[1], False)


def solution(mesh):
    placed = (P(("groups", "row"), "col", None), P(("groups", "row"), "col"), P(), P(), P())
    return jax.shard_map(
        per_device,
        mesh=mesh,
        in_specs=placed,
        out_specs=P(("groups", "row"), "col", None),
        check_vma=False,
    )
```
